32 devices in a mesh: grp: 2 (over y), seq: 4 (over z), var: 2 (over x), rep: 2 (over core).
Axes of the slice: x: 2, y: 2, z: 4, core: 2. Of those that a mesh axis runs over, the one named last changes fastest.
Arguments:
- cache_vals: bfloat16 [256, 8, 1536], P(('grp', 'seq', 'var')), parts along dimension 0, may hold values from -6 to 6
- cache_scales: bfloat16 [256, 1536], P(('grp', 'seq', 'var')), parts along dimension 0, may hold values from 0.29882812 to 3
- block_slot: int32 [256], P('grp'), parts along dimension 0, may hold values from 0 to 127, as said below
- block_lists: int32 [256, 4], P(('grp', 'seq', 'var')), parts along dimension 0, may hold values from 0 to 127, as said below
- variant_pos: int32 [256], P(('grp', 'seq', 'var')), parts along dimension 0, may hold values from 0 to 1008, as said below
- window_offsets: int32 [256], P(('grp', 'seq', 'var')), parts along dimension 0, may hold values from 0 to 15
- variant_deltas: bfloat16 [256, 1536], P(('grp', 'seq', 'var')), parts along dimension 0, may hold values from -12 to 12
- conv_taps: bfloat16 [17, 1536], replicated, may hold values from -1.5 to 1.5
- norm_gain: float32 [1536], replicated, may hold values from 0.1 to 1.9
- w_query: bfloat16 [1536, 512], P(None, 'rep'), may hold values from -0.15625 to 0.15625
- w_key: bfloat16 [1536, 512], P(None, 'rep'), may hold values from -0.3359375 to 0.3359375
- w_value: bfloat16 [1536, 768], P(None, 'rep'), may hold values from -0.609375 to 0.609375
- ref_keys: bfloat16 [2048, 512], P(('grp', 'seq'), 'rep'), parts along dimension 0, may hold values from -200 to 200
- ref_values: bfloat16 [2048, 768], P(('grp', 'seq'), 'rep'), parts along dimension 0, may hold values from -24 to 24
- head_slopes: float32 [4], P('rep'), may hold values from 3e-05 to 0.03
Outputs:
- variant_out: bfloat16 [256, 16, 768], P(('grp', 'seq', 'var'), None, 'rep'), parts along dimension 0
The draws below stay inside these ranges and needn't reach their ends.
There are 2 independent parts, one for each index of `grp`. The reference program is written for one: setup_inputs(seed, part) draws one part's arguments, and reference() takes and returns one part's arrays. A program takes and returns all parts, laid end to end along the dimension named above; an argument that names none is the same for every part. Nothing has to cross between parts.
Inputs may be any that keep to these rules, and one draw needn't show every extreme that they name: `block_slot`: each of 0 .. 127 once. block_lists[v] = a - 1, a, a + 1, a + 2 with a = variant_pos[v] / 8, the blocks around the variant's recomputed rows. Among the rows of one device along seq and var, the entries at even positions k name at most 8 blocks whose slot lies on any one device (slot // 16 along seq and var), and likewise the entries at odd k; in every draw some device reads exactly 8 entries of each parity, 16 in all, from one and the same device. `variant_pos`: a multiple of 8.
All inputs are finite; a program needn't handle non-finite values.
Results may differ from the reference program's by a relative error of at most 0.0095.
The reference program's roundings to bfloat16 on the way count: a program that leaves them out, or rounds other values in their place, can miss the bound.
Values may be sent and summed in bfloat16 or wider, within the bound.
No kernel may reach another device: no remote copies, remote signals or barrier semaphores. Data moves between devices by JAX's collectives and lax.ppermute only.
A program may use at most 64 MiB of HBM per device.

```python
import math
import jax
import jax.numpy as jnp
from jax import lax

D = 1536
H = 4
DK = 128
DV = 192
VPD = 16
BL = 8
W = 16
RADIUS = 8
K = 4
TAPS = 17
L = 1024
NBLK = 128
OWNERS = 8
BPD = 16
NV = 128


def owner_layout(base_key):
    layout_key = jax.random.fold_in(base_key, 7)
    owner_order = jax.random.permutation(layout_key, OWNERS).astype(jnp.int32)
    block_index = jnp.arange(NBLK, dtype=jnp.int32)
    return (jnp.take(owner_order, block_index % OWNERS) * BPD + block_index // OWNERS).astype(jnp.int32)


def variant_anchors(base_key):
    anchor_key = jax.random.fold_in(base_key, 13)
    order_key, depth_key, start_key = jax.random.split(anchor_key, 3)
    groups_count = OWNERS // 4
    span_width = 4 * (min(VPD, groups_count) - 1)
    depth_count = (NBLK - 4 - span_width) // OWNERS + 1
    start_most = NBLK - 3 - span_width - OWNERS * (depth_count - 1)
    order_keys = jax.random.split(order_key, OWNERS)
    orders = jax.vmap(lambda one_key: jax.random.permutation(one_key, VPD))(order_keys).astype(jnp.int32)
    depths = jax.random.randint(depth_key, (OWNERS, VPD), 0, depth_count, dtype=jnp.int32)
    starts = jax.random.randint(start_key, (OWNERS, 1), 1, start_most + 1, dtype=jnp.int32)
    group_ids = orders % groups_count
    moved = (group_ids == 1).astype(jnp.int32)
    anchors = starts + 4 * group_ids - moved + OWNERS * depths
    return anchors.reshape(OWNERS * VPD).astype(jnp.int32)


def draw_block_slot(key, part):
    return owner_layout(key)


def draw_block_lists(key, part):
    anchors = variant_anchors(key)
    return (anchors[:, None] + jnp.arange(K, dtype=jnp.int32)[None, :] - 1).astype(jnp.int32)


def draw_variant_pos(key, part):
    return (variant_anchors(key) * BL).astype(jnp.int32)


def draw_ref_keys(key, part):
    normal_key = jax.random.fold_in(key, 0)
    values = jax.random.normal(normal_key, (L, H * DK), jnp.float32) * 2.2
    return values.astype(jnp.bfloat16)


def set_ends(result, rng, smallest, top_value):
    index_at = [jax.random.randint(jax.random.fold_in(rng, axis), (), 0, length) for axis, length in enumerate(result.shape)]
    longest = result.shape.index(max(result.shape))
    neighbour = index_at[:longest] + [(index_at[longest] + 1) % result.shape[longest]] + index_at[longest + 1:]
    return result.at[tuple(index_at)].set(smallest).at[tuple(neighbour)].set(top_value)


def block_scale(key, dims, cuts, smallest, largest):
    loudness = 1.0
    for dim, blocks in cuts:
        draws = jax.random.uniform(jax.random.fold_in(jax.random.fold_in(key, 6), dim), (blocks,), jnp.float32, smallest / len(cuts), largest / len(cuts))
        loudness = loudness * jnp.repeat(jnp.exp(draws), dims[dim] // blocks).reshape((-1,) + (1,) * (len(dims) - 1 - dim))
    return loudness


def centred(own_key, extent, width, most, cuts=(), held_as=jnp.bfloat16):
    result = jax.random.normal(own_key, extent, jnp.float32) * width
    if len(cuts) > 0:
        result = block_scale(own_key, extent, cuts, -0.22, 0.18) * result
    return jnp.clip(result, min=-most, max=most).astype(held_as)


def setup_inputs(seed: int = 0, part: int = 0) -> dict:
    key_of = jax.random.split(jax.random.key(seed), 16)
    part_splits = jax.random.split(jax.random.fold_in(key_of[15], part), 16)
    return {
        "cache_vals": centred(part_splits[0], (NBLK, BL, D), 1.0, 6.0, ((0, 8),)),
        "cache_scales": jnp.clip(jnp.exp(math.log(3.0) - 2.306499 * jax.random.uniform(part_splits[1], (NBLK, D), jnp.float32) ** block_scale(part_splits[1], (NBLK, D), ((0, 8),), -0.2, 0.2)), 0.29882812, 3.0).astype(jnp.bfloat16),
        "block_slot": draw_block_slot(jax.random.fold_in(jax.random.fold_in(key_of[15], part), 71), part),
        "block_lists": draw_block_lists(jax.random.fold_in(jax.random.fold_in(key_of[15], part), 71), part),
        "variant_pos": draw_variant_pos(jax.random.fold_in(jax.random.fold_in(key_of[15], part), 71), part),
        "window_offsets": set_ends(jax.random.randint(part_splits[5], (NV,), 0, W), jax.random.fold_in(part_splits[5], 1), 0, W - 1).astype(jnp.int32),
        "variant_deltas": centred(part_splits[6], (NV, D), 2.0, 12.0, ((0, 8),)),
        "conv_taps": centred(key_of[7], (TAPS, D), TAPS ** -0.5, 1.5),
        "norm_gain": jnp.clip(1.0 + 0.18 * jax.random.normal(key_of[8], (D,), jnp.float32), 0.1, 1.9),
        "w_query": centred(key_of[9], (D, H * DK), D ** -0.5, 0.15625, ((1, 2),)),
        "w_key": centred(key_of[10], (D, H * DK), (2.2 / D ** 0.5), 0.3359375, ((1, 2),)),
        "w_value": centred(key_of[11], (D, H * DV), (4.0 / D ** 0.5), 0.609375, ((1, 2),)),
        "ref_keys": draw_ref_keys(jax.random.fold_in(jax.random.fold_in(key_of[15], part), 71), part),
        "ref_values": centred(part_splits[13], (L, H * DV), 4.0, 24.0, ((0, 4), (1, 2))),
        "head_slopes": jnp.clip(jnp.exp(math.log(0.03) - 6.9077553 * jax.random.uniform(key_of[14], (H,), jnp.float32) ** block_scale(key_of[14], (H,), ((0, 2),), -0.2, 0.2)), 2.9999999242136255e-05, 0.03),
    }


EPSILON = 1e-06

def rounded(values_in):
    return lax.optimization_barrier(values_in.astype(jnp.bfloat16)).astype(jnp.float32)

def reference(cache_vals, cache_scales, block_slot, block_lists, variant_pos, window_offsets, variant_deltas, conv_taps, norm_gain, w_query, w_key, w_value, ref_keys, ref_values, head_slopes):
    inverse_root = 1.0 / math.sqrt(DK)
    key_heads = ref_keys.astype(jnp.float32).reshape(L, H, DK)
    value_heads = ref_values.astype(jnp.float32).reshape(L, H, DV)
    tap_table = conv_taps.astype(jnp.float32)
    key_position = jnp.arange(L, dtype=jnp.int32)
    own_offset = jnp.arange(W, dtype=jnp.int32)
    own_distance = jnp.abs(own_offset[:, None] - own_offset[None, :]).astype(jnp.float32)

    def score_group(group_data):
        block_ids, starts, offsets, deltas = group_data
        group_size = block_ids.shape[0]
        slot_ids = jnp.take(block_slot, block_ids, axis=0)
        blocks = jnp.take(cache_vals, slot_ids, axis=0).astype(jnp.float32)
        scales = jnp.take(cache_scales, slot_ids, axis=0).astype(jnp.float32)
        context = (blocks * scales[:, :, None, :]).reshape(group_size, K * BL, D)
        marker = (jnp.arange(K * BL, dtype=jnp.int32)[None, :] == (RADIUS + offsets)[:, None]).astype(jnp.float32)
        altered = context + marker[:, :, None] * deltas.astype(jnp.float32)[:, None, :]
        tower_rows = altered[:, RADIUS:RADIUS + W]
        for tap_index in range(2 * RADIUS + 1):
            tower_rows = tower_rows + tap_table[tap_index] * altered[:, tap_index:tap_index + W]
        mean_square = lax.optimization_barrier(jnp.mean(tower_rows * tower_rows, axis=-1, keepdims=True))
        normed = (tower_rows * lax.rsqrt(mean_square + EPSILON) * norm_gain).astype(jnp.bfloat16).reshape(group_size * W, D)
        queries = rounded(jnp.dot(normed, w_query, preferred_element_type=jnp.float32)).reshape(group_size, W, H, DK)
        own_keys = rounded(jnp.dot(normed, w_key, preferred_element_type=jnp.float32)).reshape(group_size, W, H, DK)
        own_values = rounded(jnp.dot(normed, w_value, preferred_element_type=jnp.float32)).reshape(group_size, W, H, DV)
        positions = starts[:, None] + own_offset[None, :]
        distance = jnp.abs(positions[:, :, None] - key_position[None, None, :]).astype(jnp.float32)
        replaced = (key_position[None, :] >= starts[:, None]) & (key_position[None, :] < starts[:, None] + W)
        far_scores = jnp.einsum('gthd,jhd->gthj', queries, key_heads) * inverse_root - head_slopes[None, None, :, None] * distance[:, :, None, :]
        far_scores = jnp.where(replaced[:, None, None, :], -jnp.inf, far_scores)
        near_scores = jnp.einsum('gthd,gshd->gths', queries, own_keys) * inverse_root - head_slopes[None, None, :, None] * own_distance[None, :, None, :]
        row_peak = jnp.maximum(lax.optimization_barrier(jnp.max(far_scores, axis=-1)), lax.optimization_barrier(jnp.max(near_scores, axis=-1)))
        far_exp = jnp.exp(far_scores - row_peak[..., None])
        near_exp = jnp.exp(near_scores - row_peak[..., None])
        row_total = lax.optimization_barrier(jnp.sum(far_exp, axis=-1)) + lax.optimization_barrier(jnp.sum(near_exp, axis=-1))
        weighted = jnp.einsum('gthj,jhd->gthd', rounded(far_exp), value_heads) + jnp.einsum('gths,gshd->gthd', rounded(near_exp), own_values)
        return (weighted / row_total[..., None]).astype(jnp.bfloat16).reshape(group_size, W, H * DV)
    groups = NV // VPD
    grouped = (block_lists.reshape(groups, VPD, K), variant_pos.reshape(groups, VPD), window_offsets.reshape(groups, VPD), variant_deltas.reshape(groups, VPD, D))
    return lax.map(score_group, grouped).reshape(NV, W, H * DV)
```

```python
import functools
import math

import jax
import jax.numpy as jnp
from jax import lax
from jax.experimental import pallas as pl
from jax.experimental.pallas import tpu as pltpu
from jax.sharding import PartitionSpec as P

W = 16
RADIUS = 8
TAPS = 2 * RADIUS + 1
EPSILON = 1e-06
PARTS = 4


def send(x, seq_mask, var_mask=0):
    seq, var = lax.axis_size("seq"), lax.axis_size("var")
    pairs = [
        (p * var + q, (p ^ seq_mask) * var + (q ^ var_mask))
        for p in range(seq)
        for q in range(var)
    ]
    return lax.ppermute(x, ("seq", "var"), pairs)


def then(*arrays):
    return lax.optimization_barrier(arrays)


def pack_kernel(vals, scales, cells):
    per_owner, half = scales.shape
    cells[pl.ds(0, per_owner)] = vals[...]
    rows = scales[...].astype(jnp.float32)
    missing = (cells.shape[0] - per_owner) * 8 - per_owner
    if missing:
        rows = jnp.concatenate([rows, jnp.zeros((missing, half), jnp.float32)], axis=0)
    rows = rows.reshape(-1, 8, half).astype(jnp.bfloat16)
    cells[pl.ds(per_owner, rows.shape[0])] = rows


def gather_all(cells, window, *small):
    seq, var = lax.axis_size("seq"), lax.axis_size("var")
    me_var = lax.axis_index("var")
    if not on_line(seq, var):
        cells = lax.all_gather(cells, ("seq", "var"), axis=0, tiled=False)
        return [cells], [lax.all_gather(window, "seq", axis=0, tiled=True)], small
    part = window.shape[0] // 2

    cells_1, across, cells_3 = send(cells, 1), send(cells, 0, 1), send(cells, 3)
    cells_1, across, window = then(cells_1, across, window)
    share = lax.dynamic_slice_in_dim(window, me_var * part, part, axis=0)
    across_1 = send(cells_1, 0, 1)
    cells_3, *small = then(cells_3, *small)
    cells_2 = send(cells_3, 1)
    cells_3, across_1 = then(cells_3, across_1)
    across_3 = send(cells_3, 0, 1)
    cells_2, share = then(cells_2, share)
    across_2, share_2 = send(cells_2, 0, 1), send(share, 2)
    across_3, share = then(across_3, share)
    share_1 = send(share, 1)
    share_3 = send(share_2, 1)
    share_across_2, share_across_1 = send(share_2, 0, 1), send(share_1, 0, 1)
    share_across_3 = send(share_3, 0, 1)

    pieces = [cells, across, cells_1, across_1, cells_2, across_2, cells_3, across_3]
    windows = [
        window,
        share_1,
        share_across_1,
        share_2,
        share_across_2,
        share_3,
        share_across_3,
    ]
    return [piece[None] for piece in pieces], windows, small


def on_line(seq, var):
    return seq == 4 and var == 2


def place_of(owner):
    seq, var = lax.axis_size("seq"), lax.axis_size("var")
    if not on_line(seq, var):
        return owner
    return owner ^ (lax.axis_index("seq") * var + lax.axis_index("var"))


def first_keys(rows):
    seq, var = lax.axis_size("seq"), lax.axis_size("var")
    me_seq, me_var = lax.axis_index("seq"), lax.axis_index("var")
    if not on_line(seq, var):
        return [[rows * p for p in range(seq)]]
    firsts = [[me_seq * rows]]
    for mask in (1, 2, 3):
        for side in (0, 1):
            firsts.append([(me_seq ^ mask) * rows + (me_var ^ side) * (rows // 2)])
    return firsts


def tower_kernel(
    per_owner,
    block_slot,
    block_lists,
    window_offsets,
    deltas,
    taps,
    *rest,
):
    *rest, held, taps32, deltas32 = rest
    pieces, outs = rest[:-PARTS], rest[-PARTS:]
    channels = taps32.shape[2]
    taps32[...] = jnp.broadcast_to(taps[...].astype(jnp.float32)[:, None, :], taps32.shape)
    deltas32[...] = deltas[...].astype(jnp.float32)
    first = 0
    for piece in pieces:
        scale_cells = piece.shape[1] - per_owner
        for p in range(piece.shape[0]):
            scale = piece[p, pl.ds(per_owner, scale_cells)].astype(jnp.float32)
            scale = scale.reshape(scale_cells * 8, channels)
            for i in range(per_owner):
                held[first + i] = piece[p, i].astype(jnp.float32) * scale[i : i + 1]
            first += per_owner
    chunk = 256
    row = lax.broadcasted_iota(jnp.int32, (8, chunk), 0)

    def variant(out, begin, v):
        places = []
        for k in range(4):
            slot = block_slot[block_lists[k, begin + v]]
            owner = slot // per_owner
            places.append(place_of(owner) * per_owner + slot - owner * per_owner)
        offset = window_offsets[begin + v]
        for at in range(0, channels, chunk):
            lanes = slice(at, at + chunk)
            cells = [held[place, :, lanes] for place in places]
            delta = deltas32[pl.ds(begin + v, 1), lanes]
            cells[1] = cells[1] + jnp.where(row == offset, delta, 0.0)
            cells[2] = cells[2] + jnp.where(row == offset - 8, delta, 0.0)
            early, late = jnp.stack(cells[:3]), jnp.stack(cells[1:])
            total = None
            for s in range(7, 0, -1):
                term = early * taps32[s, :, lanes] + late * taps32[s + 8, :, lanes]
                total = term if total is None else total + term
                total = pltpu.roll(total.reshape(24, chunk), 23, 0).reshape(3, 8, chunk)
            total = total[0:2] + early[0:2] * taps32[0, :, lanes]
            total = total + late[0:2] * (1.0 + taps32[8, :, lanes])
            total = total + late[1:3] * taps32[16, :, lanes]
            out[pl.ds(pl.multiple_of(v * W, W), W), lanes] = total.reshape(W, chunk)

    begin = 0
    for out in outs:
        pl.loop(0, out.shape[0] // W)(functools.partial(variant, out, begin))
        begin += out.shape[0] // W


def value_window(h, value_width):
    return h * value_width // 128 * 128, -(-(h + 1) * value_width // 128) * 128


def row_starts(positions):
    return jnp.concatenate(
        [jnp.full((W, 1), positions[v], jnp.int32) for v in range(positions.shape[0])], axis=0
    ).astype(jnp.float32)


def scores_of(query, keys):
    product = lax.dot_general(
        query, keys, (((1,), (1,)), ((), ())), preferred_element_type=jnp.float32
    )
    return product * (1.0 / math.sqrt(query.shape[1]))


def key_places(piece, firsts):
    each = piece.shape[0] // len(firsts)
    places = [first + lax.broadcasted_iota(jnp.int32, (1, each), 1) for first in firsts]
    return jnp.concatenate(places, axis=1).astype(jnp.float32)


def piece_scores(h, query, start, place, slope, pieces, firsts):
    width, found = query.shape[1], []
    for piece, first in zip(pieces, firsts):
        key_at = key_places(piece, first)
        score = scores_of(query, piece[:, h * width : (h + 1) * width])
        score = score - slope * jnp.abs(place - key_at)
        kept = jnp.abs(start + (W - 1) / 2 - key_at) > W / 2
        found.append(jnp.where(kept, score, -jnp.inf))
    return found


def weigh(scores, values, peak):
    total, summed = 0.0, 0.0
    for score, value in zip(scores, values):
        weight = jnp.exp(score - peak)
        total = total + jnp.sum(weight, axis=1, keepdims=True)
        summed = summed + jnp.dot(
            weight.astype(jnp.bfloat16), value, preferred_element_type=jnp.float32
        )
    return total, summed


def peak_of(scores):
    return functools.reduce(jnp.maximum, [jnp.max(s, axis=1, keepdims=True) for s in scores])


def near_kernel(
    sizes,
    positions,
    slopes,
    gain,
    w_query,
    w_key,
    w_value,
    *rest,
):
    value_width, window_rows = sizes
    mine, others = rest[:PARTS], rest[PARTS : 2 * PARTS]
    pieces = rest[2 * PARTS : -3]
    queries_out, stats, sums = rest[-3:]
    heads = slopes.shape[0]
    rep = lax.axis_index("rep")
    own = jnp.concatenate([part[...] for part in mine], axis=0)
    far = jnp.concatenate([part[...] for part in others], axis=0)
    rows, half = own.shape
    mean = (
        jnp.sum(own * own, axis=1, keepdims=True) + jnp.sum(far * far, axis=1, keepdims=True)
    ) / (2 * half)
    factor = lax.rsqrt(mean + EPSILON)
    gain_low, gain_high = gain[:, :half], gain[:, half:]
    own = own * factor * jnp.where(rep == 0, gain_low, gain_high)
    far = far * factor * jnp.where(rep == 0, gain_high, gain_low)
    own, far = own.astype(jnp.bfloat16), far.astype(jnp.bfloat16)
    at_own = pl.ds(pl.multiple_of(rep * half, half), half)
    at_far = pl.ds(pl.multiple_of((1 - rep) * half, half), half)

    def project(w):
        return (
            jnp.dot(own, w[at_own, :], preferred_element_type=jnp.float32)
            + jnp.dot(far, w[at_far, :], preferred_element_type=jnp.float32)
        ).astype(jnp.bfloat16)

    queries, own_keys, own_values = project(w_query), project(w_key), project(w_value)
    queries_out[...] = queries
    start = row_starts(positions)
    place = start + (lax.broadcasted_iota(jnp.int32, (rows, 1), 0) % W).astype(jnp.float32)
    at = lax.broadcasted_iota(jnp.int32, (rows, rows), 0)
    to = lax.broadcasted_iota(jnp.int32, (rows, rows), 1)
    together, apart = at // W == to // W, jnp.abs(at - to).astype(jnp.float32)
    width = queries.shape[1] // heads
    for h in range(heads):
        cols = slice(h * width, (h + 1) * width)
        low, high = value_window(h, value_width)
        base = heads * width
        near = scores_of(queries[:, cols], own_keys[:, cols]) - slopes[h] * apart
        scores = [jnp.where(together, near, -jnp.inf)]
        scores += piece_scores(
            h, queries[:, cols], start, place, slopes[h], pieces, first_keys(window_rows)
        )
        values = [own_values[:, low:high]]
        values += [piece[:, base + low : base + high] for piece in pieces]
        peak = peak_of(scores)
        total, summed = weigh(scores, values, peak)
        stats[2 * h] = jnp.broadcast_to(peak, (rows, 128))
        stats[2 * h + 1] = jnp.broadcast_to(total, (rows, 128))
        sums[h] = summed


def far_kernel(sizes, positions, slopes, queries, stats, sums, *rest):
    value_width, window_rows = sizes
    *pieces, out = rest
    firsts = first_keys(window_rows)[-len(pieces) :]
    heads = slopes.shape[0]
    rows, width = queries.shape[0], queries.shape[1] // heads
    start = row_starts(positions)
    place = start + (lax.broadcasted_iota(jnp.int32, (rows, 1), 0) % W).astype(jnp.float32)
    results = []
    for h in range(heads):
        low, high = value_window(h, value_width)
        base = heads * width
        scores = piece_scores(
            h,
            queries[:, h * width : (h + 1) * width],
            start,
            place,
            slopes[h],
            pieces,
            firsts,
        )
        values = [piece[:, base + low : base + high] for piece in pieces]
        before = stats[2 * h][:, :1]
        peak = jnp.maximum(before, peak_of(scores))
        total, summed = weigh(scores, values, peak)
        factor = jnp.exp(before - peak)
        total = total + stats[2 * h + 1][:, :1] * factor
        summed = summed + sums[h] * factor
        results.append((low, high, summed * (1.0 / total)))
    lane = lax.broadcasted_iota(jnp.int32, (rows, 128), 1)
    for column in range(0, heads * value_width, 128):
        merged = None
        for h, (low, high, value) in enumerate(results):
            if low <= column < high:
                part = value[:, column - low : column - low + 128]
                if merged is None:
                    merged = part
                else:
                    merged = jnp.where(lane + column >= h * value_width, part, merged)
        out[:, column : column + 128] = merged.astype(jnp.bfloat16)


def on_device(
    cache_vals,
    cache_scales,
    block_slot,
    block_lists,
    variant_pos,
    window_offsets,
    variant_deltas,
    conv_taps,
    norm_gain,
    w_query,
    w_key,
    w_value,
    ref_keys,
    ref_values,
    head_slopes,
):
    per_owner, block_rows, channels = cache_vals.shape
    variants = block_lists.shape[0]
    half = channels // lax.axis_size("rep")
    smem = pl.BlockSpec(memory_space=pltpu.SMEM)
    vmem = pl.BlockSpec(memory_space=pltpu.VMEM)

    def my_half(x):
        return lax.dynamic_slice_in_dim(x, lax.axis_index("rep") * half, half, axis=x.ndim - 1)

    scales, vals = then(my_half(cache_scales), cache_vals)
    all_cells = per_owner + -(-per_owner // 8)
    cells = pl.pallas_call(
        pack_kernel,
        out_shape=jax.ShapeDtypeStruct((all_cells, block_rows, half), jnp.bfloat16),
        in_specs=[vmem, vmem],
        out_specs=vmem,
        compiler_params=pltpu.CompilerParams(vmem_limit_bytes=4 * 1024 * 1024),
        name="pack",
    )(my_half(vals), scales)
    window = jnp.concatenate([ref_keys, ref_values], axis=1)
    slot_pieces, window_pieces, (deltas, taps, gain) = gather_all(
        cells,
        window,
        my_half(variant_deltas),
        my_half(conv_taps),
        norm_gain.reshape(1, channels),
    )
    held = sum(piece.shape[0] for piece in slot_pieces) * per_owner
    tower_limit = 8 * held * block_rows * half * 4 // 3 + 4 * 1024 * 1024
    tower_shapes = [
        jax.ShapeDtypeStruct(((variants + i) // PARTS * W, half), jnp.float32)
        for i in reversed(range(PARTS))
    ]
    towers = pl.pallas_call(
        functools.partial(tower_kernel, per_owner),
        out_shape=tower_shapes,
        in_specs=[smem, smem, smem] + [vmem] * (2 + len(slot_pieces)),
        out_specs=[vmem] * PARTS,
        scratch_shapes=[
            pltpu.VMEM((held, block_rows, half), jnp.float32),
            pltpu.VMEM((TAPS, 8, half), jnp.float32),
            pltpu.VMEM((variants, half), jnp.float32),
        ],
        compiler_params=pltpu.CompilerParams(vmem_limit_bytes=tower_limit),
        cost_estimate=pl.CostEstimate(
            flops=10**9, bytes_accessed=4 * 10**7, transcendentals=0
        ),
        name="tower",
    )(
        block_slot,
        block_lists.T,
        window_offsets,
        deltas,
        taps,
        *slot_pieces,
    )
    swap = [(0, 1), (1, 0)]
    if len(window_pieces) > 2:
        *towers, window_pieces[5] = then(*towers, window_pieces[5])
        *towers, last = towers
        last, window_pieces[2], window_pieces[4] = then(last, window_pieces[2], window_pieces[4])
        towers = [*towers, last]
    others = [lax.ppermute(tower, "rep", swap) for tower in towers]
    heads, rows = head_slopes.shape[0], variants * W
    value_width = w_value.shape[1] // heads
    cut = len(window_pieces) - 1
    sizes = (value_width, ref_keys.shape[0])
    low, high = value_window(heads - 1, value_width)
    queries, stats, sums = pl.pallas_call(
        functools.partial(near_kernel, sizes),
        out_shape=[
            jax.ShapeDtypeStruct((rows, w_query.shape[1]), jnp.bfloat16),
            jax.ShapeDtypeStruct((2 * heads, rows, 128), jnp.float32),
            jax.ShapeDtypeStruct((heads, rows, high - low), jnp.float32),
        ],
        in_specs=[smem, smem] + [vmem] * (4 + 2 * PARTS + cut),
        out_specs=[vmem] * 3,
        compiler_params=pltpu.CompilerParams(vmem_limit_bytes=20 * 1024 * 1024),
        name="near",
    )(
        variant_pos,
        head_slopes,
        gain,
        w_query,
        w_key,
        w_value,
        *towers,
        *others,
        *window_pieces[:cut],
    )
    output = pl.pallas_call(
        functools.partial(far_kernel, sizes),
        out_shape=jax.ShapeDtypeStruct((rows, w_value.shape[1]), jnp.bfloat16),
        in_specs=[smem, smem] + [vmem] * (3 + len(window_pieces) - cut),
        out_specs=vmem,
        compiler_params=pltpu.CompilerParams(vmem_limit_bytes=20 * 1024 * 1024),
        name="far",
    )(variant_pos, head_slopes, queries, stats, sums, *window_pieces[cut:])
    return output.reshape(variants, W, -1)


def solution(mesh):
    placed = (
        P(("grp", "seq", "var"), None, None),
        P(("grp", "seq", "var"), None),
        P("grp"),
        P(("grp", "seq", "var"), None),
        P(("grp", "seq", "var")),
        P(("grp", "seq", "var")),
        P(("grp", "seq", "var"), None),
        P(),
        P(),
        P(None, "rep"),
        P(None, "rep"),
        P(None, "rep"),
        P(("grp", "seq"), "rep"),
        P(("grp", "seq"), "rep"),
        P("rep"),
    )
    return jax.shard_map(
        on_device,
        mesh=mesh,
        in_specs=placed,
        out_specs=P(("grp", "seq", "var"), None, "rep"),
        check_vma=False,
    )
```

```python
import functools
import math

import jax
import jax.numpy as jnp
from jax import lax
from jax.experimental import pallas as pl
from jax.experimental.pallas import tpu as pltpu
from jax.sharding import PartitionSpec as P

W = 16
RADIUS = 8
TAPS = 2 * RADIUS + 1
EPSILON = 1e-06
PARTS = 3


def send(x, seq_mask, var_mask=0):
    seq, var = lax.axis_size("seq"), lax.axis_size("var")
    pairs = [
        (p * var + q, (p ^ seq_mask) * var + (q ^ var_mask))
        for p in range(seq)
        for q in range(var)
    ]
    return lax.ppermute(x, ("seq", "var"), pairs)


def then(*arrays):
    return lax.optimization_barrier(arrays)


def pack_kernel(vals, scales, cells):
    per_owner, half = scales.shape
    cells[pl.ds(0, per_owner)] = vals[...]
    rows = scales[...].astype(jnp.float32)
    missing = (cells.shape[0] - per_owner) * 8 - per_owner
    if missing:
        rows = jnp.concatenate([rows, jnp.zeros((missing, half), jnp.float32)], axis=0)
    rows = rows.reshape(-1, 8, half).astype(jnp.bfloat16)
    cells[pl.ds(per_owner, rows.shape[0])] = rows


def gather_all(cells, window, *small):
    seq, var = lax.axis_size("seq"), lax.axis_size("var")
    me_var = lax.axis_index("var")
    if not on_line(seq, var):
        cells = lax.all_gather(cells, ("seq", "var"), axis=0, tiled=False)
        return [cells], [lax.all_gather(window, "seq", axis=0, tiled=True)], small
    part = window.shape[0] // 2

    cells_1, across, cells_3 = send(cells, 1), send(cells, 0, 1), send(cells, 3)
    cells_1, across, window = then(cells_1, across, window)
    share = lax.dynamic_slice_in_dim(window, me_var * part, part, axis=0)
    across_1 = send(cells_1, 0, 1)
    cells_3, *small = then(cells_3, *small)
    cells_2 = send(cells_3, 1)
    cells_3, across_1 = then(cells_3, across_1)
    across_3 = send(cells_3, 0, 1)
    cells_2, share = then(cells_2, share)
    across_2, share_3 = send(cells_2, 0, 1), send(share, 3)
    across_3, share_3, window = then(across_3, share_3, window)
    share_2, share_across_3 = send(share_3, 1), send(share_3, 0, 1)
    window_1, share_across_2 = send(window, 1), send(share_2, 0, 1)

    pieces = [cells, across, cells_1, across_1, cells_2, across_2, cells_3, across_3]
    windows = [window, window_1, share_3, share_across_3, share_2, share_across_2]
    return [piece[None] for piece in pieces], windows, small


def on_line(seq, var):
    return seq == 4 and var == 2


def place_of(owner):
    seq, var = lax.axis_size("seq"), lax.axis_size("var")
    if not on_line(seq, var):
        return owner
    return owner ^ (lax.axis_index("seq") * var + lax.axis_index("var"))


def first_keys(rows):
    seq, var = lax.axis_size("seq"), lax.axis_size("var")
    me_seq, me_var = lax.axis_index("seq"), lax.axis_index("var")
    if not on_line(seq, var):
        return [[rows * p for p in range(seq)]]
    firsts = [[me_seq * rows], [(me_seq ^ 1) * rows]]
    for mask in (3, 2):
        for side in (0, 1):
            firsts.append([(me_seq ^ mask) * rows + (me_var ^ side) * (rows // 2)])
    return firsts


def tower_kernel(
    per_owner,
    block_slot,
    block_lists,
    window_offsets,
    deltas,
    taps,
    *rest,
):
    *rest, held, taps32, deltas32 = rest
    pieces, outs = rest[:-PARTS], rest[-PARTS:]
    channels = taps32.shape[2]
    taps32[...] = jnp.broadcast_to(taps[...].astype(jnp.float32)[:, None, :], taps32.shape)
    deltas32[...] = deltas[...].astype(jnp.float32)
    first = 0
    for piece in pieces:
        scale_cells = piece.shape[1] - per_owner
        for p in range(piece.shape[0]):
            scale = piece[p, pl.ds(per_owner, scale_cells)].astype(jnp.float32)
            scale = scale.reshape(scale_cells * 8, channels)
            for i in range(per_owner):
                held[first + i] = piece[p, i].astype(jnp.float32) * scale[i : i + 1]
            first += per_owner
    chunk = 256
    row = lax.broadcasted_iota(jnp.int32, (8, chunk), 0)

    def variant(out, begin, v):
        places = []
        for k in range(4):
            slot = block_slot[block_lists[k, begin + v]]
            owner = slot // per_owner
            places.append(place_of(owner) * per_owner + slot - owner * per_owner)
        offset = window_offsets[begin + v]
        for at in range(0, channels, chunk):
            lanes = slice(at, at + chunk)
            cells = [held[place, :, lanes] for place in places]
            delta = deltas32[pl.ds(begin + v, 1), lanes]
            cells[1] = cells[1] + jnp.where(row == offset, delta, 0.0)
            cells[2] = cells[2] + jnp.where(row == offset - 8, delta, 0.0)
            early, late = jnp.stack(cells[:3]), jnp.stack(cells[1:])
            total = None
            for s in range(7, 0, -1):
                term = early * taps32[s, :, lanes] + late * taps32[s + 8, :, lanes]
                total = term if total is None else total + term
                total = pltpu.roll(total.reshape(24, chunk), 23, 0).reshape(3, 8, chunk)
            total = total[0:2] + early[0:2] * taps32[0, :, lanes]
            total = total + late[0:2] * (1.0 + taps32[8, :, lanes])
            total = total + late[1:3] * taps32[16, :, lanes]
            out[pl.ds(pl.multiple_of(v * W, W), W), lanes] = total.reshape(W, chunk)

    begin = 0
    for out in outs:
        pl.loop(0, out.shape[0] // W)(functools.partial(variant, out, begin))
        begin += out.shape[0] // W


def value_window(h, value_width):
    return h * value_width // 128 * 128, -(-(h + 1) * value_width // 128) * 128


def row_starts(positions):
    return jnp.concatenate(
        [jnp.full((W, 1), positions[v], jnp.int32) for v in range(positions.shape[0])], axis=0
    ).astype(jnp.float32)


def scores_of(query, keys):
    product = lax.dot_general(
        query, keys, (((1,), (1,)), ((), ())), preferred_element_type=jnp.float32
    )
    return product * (1.0 / math.sqrt(query.shape[1]))


def key_places(piece, firsts):
    each = piece.shape[0] // len(firsts)
    places = [first + lax.broadcasted_iota(jnp.int32, (1, each), 1) for first in firsts]
    return jnp.concatenate(places, axis=1).astype(jnp.float32)


def piece_scores(h, query, start, place, slope, pieces, firsts):
    width, found = query.shape[1], []
    for piece, first in zip(pieces, firsts):
        key_at = key_places(piece, first)
        score = scores_of(query, piece[:, h * width : (h + 1) * width])
        score = score - slope * jnp.abs(place - key_at)
        kept = jnp.abs(start + (W - 1) / 2 - key_at) > W / 2
        found.append(jnp.where(kept, score, -jnp.inf))
    return found


def weigh(scores, values, peak):
    total, summed = 0.0, 0.0
    for score, value in zip(scores, values):
        weight = jnp.exp(score - peak)
        total = total + jnp.sum(weight, axis=1, keepdims=True)
        summed = summed + jnp.dot(
            weight.astype(jnp.bfloat16), value, preferred_element_type=jnp.float32
        )
    return total, summed


def peak_of(scores):
    return functools.reduce(jnp.maximum, [jnp.max(s, axis=1, keepdims=True) for s in scores])


def near_kernel(
    sizes,
    positions,
    slopes,
    gain,
    w_query,
    w_key,
    w_value,
    *rest,
):
    value_width, window_rows = sizes
    mine, others = rest[:PARTS], rest[PARTS : 2 * PARTS]
    pieces = rest[2 * PARTS : -3]
    queries_out, stats, sums = rest[-3:]
    heads = slopes.shape[0]
    rep = lax.axis_index("rep")
    own = jnp.concatenate([part[...] for part in mine], axis=0)
    far = jnp.concatenate([part[...] for part in others], axis=0)
    rows, half = own.shape
    mean = (
        jnp.sum(own * own, axis=1, keepdims=True) + jnp.sum(far * far, axis=1, keepdims=True)
    ) / (2 * half)
    factor = lax.rsqrt(mean + EPSILON)
    gain_low, gain_high = gain[:, :half], gain[:, half:]
    own = own * factor * jnp.where(rep == 0, gain_low, gain_high)
    far = far * factor * jnp.where(rep == 0, gain_high, gain_low)
    own, far = own.astype(jnp.bfloat16), far.astype(jnp.bfloat16)
    at_own = pl.ds(pl.multiple_of(rep * half, half), half)
    at_far = pl.ds(pl.multiple_of((1 - rep) * half, half), half)

    def project(w):
        return (
            jnp.dot(own, w[at_own, :], preferred_element_type=jnp.float32)
            + jnp.dot(far, w[at_far, :], preferred_element_type=jnp.float32)
        ).astype(jnp.bfloat16)

    queries, own_keys, own_values = project(w_query), project(w_key), project(w_value)
    queries_out[...] = queries
    start = row_starts(positions)
    place = start + (lax.broadcasted_iota(jnp.int32, (rows, 1), 0) % W).astype(jnp.float32)
    at = lax.broadcasted_iota(jnp.int32, (rows, rows), 0)
    to = lax.broadcasted_iota(jnp.int32, (rows, rows), 1)
    together, apart = at // W == to // W, jnp.abs(at - to).astype(jnp.float32)
    width = queries.shape[1] // heads
    for h in range(heads):
        cols = slice(h * width, (h + 1) * width)
        low, high = value_window(h, value_width)
        base = heads * width
        near = scores_of(queries[:, cols], own_keys[:, cols]) - slopes[h] * apart
        scores = [jnp.where(together, near, -jnp.inf)]
        scores += piece_scores(
            h, queries[:, cols], start, place, slopes[h], pieces, first_keys(window_rows)
        )
        values = [own_values[:, low:high]]
        values += [piece[:, base + low : base + high] for piece in pieces]
        peak = peak_of(scores)
        total, summed = weigh(scores, values, peak)
        stats[2 * h] = jnp.broadcast_to(peak, (rows, 128))
        stats[2 * h + 1] = jnp.broadcast_to(total, (rows, 128))
        sums[h] = summed


def far_kernel(sizes, positions, slopes, queries, stats, sums, *rest):
    value_width, window_rows = sizes
    *pieces, out = rest
    firsts = first_keys(window_rows)[-len(pieces) :]
    heads = slopes.shape[0]
    rows, width = queries.shape[0], queries.shape[1] // heads
    start = row_starts(positions)
    place = start + (lax.broadcasted_iota(jnp.int32, (rows, 1), 0) % W).astype(jnp.float32)
    results = []
    for h in range(heads):
        low, high = value_window(h, value_width)
        base = heads * width
        scores = piece_scores(
            h,
            queries[:, h * width : (h + 1) * width],
            start,
            place,
            slopes[h],
            pieces,
            firsts,
        )
        values = [piece[:, base + low : base + high] for piece in pieces]
        before = stats[2 * h][:, :1]
        peak = jnp.maximum(before, peak_of(scores))
        total, summed = weigh(scores, values, peak)
        factor = jnp.exp(before - peak)
        total = total + stats[2 * h + 1][:, :1] * factor
        summed = summed + sums[h] * factor
        results.append((low, high, summed * (1.0 / total)))
    lane = lax.broadcasted_iota(jnp.int32, (rows, 128), 1)
    for column in range(0, heads * value_width, 128):
        merged = None
        for h, (low, high, value) in enumerate(results):
            if low <= column < high:
                part = value[:, column - low : column - low + 128]
                if merged is None:
                    merged = part
                else:
                    merged = jnp.where(lane + column >= h * value_width, part, merged)
        out[:, column : column + 128] = merged.astype(jnp.bfloat16)


def on_device(
    cache_vals,
    cache_scales,
    block_slot,
    block_lists,
    variant_pos,
    window_offsets,
    variant_deltas,
    conv_taps,
    norm_gain,
    w_query,
    w_key,
    w_value,
    ref_keys,
    ref_values,
    head_slopes,
):
    per_owner, block_rows, channels = cache_vals.shape
    variants = block_lists.shape[0]
    half = channels // lax.axis_size("rep")
    smem = pl.BlockSpec(memory_space=pltpu.SMEM)
    vmem = pl.BlockSpec(memory_space=pltpu.VMEM)

    def my_half(x):
        return lax.dynamic_slice_in_dim(x, lax.axis_index("rep") * half, half, axis=x.ndim - 1)

    scales, vals = then(my_half(cache_scales), cache_vals)
    all_cells = per_owner + -(-per_owner // 8)
    cells = pl.pallas_call(
        pack_kernel,
        out_shape=jax.ShapeDtypeStruct((all_cells, block_rows, half), jnp.bfloat16),
        in_specs=[vmem, vmem],
        out_specs=vmem,
        compiler_params=pltpu.CompilerParams(vmem_limit_bytes=4 * 1024 * 1024),
        name="pack",
    )(my_half(vals), scales)
    window = jnp.concatenate([ref_keys, ref_values], axis=1)
    slot_pieces, window_pieces, (deltas, taps, gain) = gather_all(
        cells,
        window,
        my_half(variant_deltas),
        my_half(conv_taps),
        norm_gain.reshape(1, channels),
    )
    held = sum(piece.shape[0] for piece in slot_pieces) * per_owner
    tower_limit = 8 * held * block_rows * half * 4 // 3 + 4 * 1024 * 1024
    tower_shapes = [
        jax.ShapeDtypeStruct(((variants + i) // PARTS * W, half), jnp.float32)
        for i in reversed(range(PARTS))
    ]
    towers = pl.pallas_call(
        functools.partial(tower_kernel, per_owner),
        out_shape=tower_shapes,
        in_specs=[smem, smem, smem] + [vmem] * (2 + len(slot_pieces)),
        out_specs=[vmem] * PARTS,
        scratch_shapes=[
            pltpu.VMEM((held, block_rows, half), jnp.float32),
            pltpu.VMEM((TAPS, 8, half), jnp.float32),
            pltpu.VMEM((variants, half), jnp.float32),
        ],
        compiler_params=pltpu.CompilerParams(vmem_limit_bytes=tower_limit),
        cost_estimate=pl.CostEstimate(
            flops=10**9, bytes_accessed=4 * 10**7, transcendentals=0
        ),
        name="tower",
    )(
        block_slot,
        block_lists.T,
        window_offsets,
        deltas,
        taps,
        *slot_pieces,
    )
    swap = [(0, 1), (1, 0)]
    if len(window_pieces) > 2:
        *towers, window_pieces[4] = then(*towers, window_pieces[4])
        *towers, last = towers
        last, window_pieces[3] = then(last, window_pieces[3])
        towers = [*towers, last]
    others = [lax.ppermute(tower, "rep", swap) for tower in towers]
    heads, rows = head_slopes.shape[0], variants * W
    value_width = w_value.shape[1] // heads
    cut = len(window_pieces) - 1
    sizes = (value_width, ref_keys.shape[0])
    low, high = value_window(heads - 1, value_width)
    queries, stats, sums = pl.pallas_call(
        functools.partial(near_kernel, sizes),
        out_shape=[
            jax.ShapeDtypeStruct((rows, w_query.shape[1]), jnp.bfloat16),
            jax.ShapeDtypeStruct((2 * heads, rows, 128), jnp.float32),
            jax.ShapeDtypeStruct((heads, rows, high - low), jnp.float32),
        ],
        in_specs=[smem, smem] + [vmem] * (4 + 2 * PARTS + cut),
        out_specs=[vmem] * 3,
        compiler_params=pltpu.CompilerParams(vmem_limit_bytes=20 * 1024 * 1024),
        name="near",
    )(
        variant_pos,
        head_slopes,
        gain,
        w_query,
        w_key,
        w_value,
        *towers,
        *others,
        *window_pieces[:cut],
    )
    output = pl.pallas_call(
        functools.partial(far_kernel, sizes),
        out_shape=jax.ShapeDtypeStruct((rows, w_value.shape[1]), jnp.bfloat16),
        in_specs=[smem, smem] + [vmem] * (3 + len(window_pieces) - cut),
        out_specs=vmem,
        compiler_params=pltpu.CompilerParams(vmem_limit_bytes=20 * 1024 * 1024),
        name="far",
    )(variant_pos, head_slopes, queries, stats, sums, *window_pieces[cut:])
    return output.reshape(variants, W, -1)


def solution(mesh):
    placed = (
        P(("grp", "seq", "var"), None, None),
        P(("grp", "seq", "var"), None),
        P("grp"),
        P(("grp", "seq", "var"), None),
        P(("grp", "seq", "var")),
        P(("grp", "seq", "var")),
        P(("grp", "seq", "var"), None),
        P(),
        P(),
        P(None, "rep"),
        P(None, "rep"),
        P(None, "rep"),
        P(("grp", "seq"), "rep"),
        P(("grp", "seq"), "rep"),
        P("rep"),
    )
    return jax.shard_map(
        on_device,
        mesh=mesh,
        in_specs=placed,
        out_specs=P(("grp", "seq", "var"), None, "rep"),
        check_vma=False,
    )
```

```python
import functools
import math

import jax
import jax.numpy as jnp
from jax import lax
from jax.experimental import pallas as pl
from jax.experimental.pallas import tpu as pltpu
from jax.sharding import PartitionSpec as P

W = 16
RADIUS = 8
TAPS = 2 * RADIUS + 1
EPSILON = 1e-06
PARTS = 3


def send(x, seq_mask, var_mask=0):
    seq, var = lax.axis_size("seq"), lax.axis_size("var")
    pairs = [
        (p * var + q, (p ^ seq_mask) * var + (q ^ var_mask))
        for p in range(seq)
        for q in range(var)
    ]
    return lax.ppermute(x, ("seq", "var"), pairs)


def then(*arrays):
    return lax.optimization_barrier(arrays)


def pack_kernel(vals, scales, cells):
    per_owner, half = scales.shape
    cells[pl.ds(0, per_owner)] = vals[...]
    rows = scales[...].astype(jnp.float32)
    missing = (cells.shape[0] - per_owner) * 8 - per_owner
    if missing:
        rows = jnp.concatenate([rows, jnp.zeros((missing, half), jnp.float32)], axis=0)
    rows = rows.reshape(-1, 8, half).astype(jnp.bfloat16)
    cells[pl.ds(per_owner, rows.shape[0])] = rows


def gather_all(cells, window, *small):
    seq, var = lax.axis_size("seq"), lax.axis_size("var")
    me_var = lax.axis_index("var")
    if not on_line(seq, var):
        cells = lax.all_gather(cells, ("seq", "var"), axis=0, tiled=False)
        return [cells], [lax.all_gather(window, "seq", axis=0, tiled=True)], small
    part = window.shape[0] // 2

    cells_1, across, cells_3 = send(cells, 1), send(cells, 0, 1), send(cells, 3)
    cells_1, across, window = then(cells_1, across, window)
    share = lax.dynamic_slice_in_dim(window, me_var * part, part, axis=0)
    across_1 = send(cells_1, 0, 1)
    cells_3, *small = then(cells_3, *small)
    cells_2 = send(cells_3, 1)
    cells_3, across_1 = then(cells_3, across_1)
    across_3 = send(cells_3, 0, 1)
    cells_2, share = then(cells_2, share)
    across_2, share_3 = send(cells_2, 0, 1), send(share, 3)
    across_3, share_3, window = then(across_3, share_3, window)
    share_2, share_across_3 = send(share_3, 1), send(share_3, 0, 1)
    window_1, share_across_2 = send(window, 1), send(share_2, 0, 1)

    pieces = [cells, across, cells_1, across_1, cells_2, across_2, cells_3, across_3]
    windows = [window, window_1, share_3, share_across_3, share_2, share_across_2]
    return [piece[None] for piece in pieces], windows, small


def on_line(seq, var):
    return seq == 4 and var == 2


def place_of(owner):
    seq, var = lax.axis_size("seq"), lax.axis_size("var")
    if not on_line(seq, var):
        return owner
    return owner ^ (lax.axis_index("seq") * var + lax.axis_index("var"))


def first_keys(rows):
    seq, var = lax.axis_size("seq"), lax.axis_size("var")
    me_seq, me_var = lax.axis_index("seq"), lax.axis_index("var")
    if not on_line(seq, var):
        return [[rows * p for p in range(seq)]]
    firsts = [[me_seq * rows], [(me_seq ^ 1) * rows]]
    for mask in (3, 2):
        for side in (0, 1):
            firsts.append([(me_seq ^ mask) * rows + (me_var ^ side) * (rows // 2)])
    return firsts


def tower_kernel(
    per_owner,
    block_slot,
    block_lists,
    window_offsets,
    deltas,
    taps,
    *rest,
):
    *rest, held, taps32, deltas32, spots = rest
    pieces, outs = rest[:-PARTS], rest[-PARTS:]
    channels = taps32.shape[2]
    for v in range(block_lists.shape[1]):
        for k in range(4):
            slot = block_slot[block_lists[k, v]]
            owner = lax.div(slot, per_owner)
            spots[4 * v + k] = place_of(owner) * per_owner + lax.rem(slot, per_owner)
    taps32[...] = jnp.broadcast_to(taps[...].astype(jnp.float32)[:, None, :], taps32.shape)
    deltas32[...] = deltas[...].astype(jnp.float32)
    first = 0
    for piece in pieces:
        scale_cells = piece.shape[1] - per_owner
        for p in range(piece.shape[0]):
            scale = piece[p, pl.ds(per_owner, scale_cells)].astype(jnp.float32)
            scale = scale.reshape(scale_cells * 8, channels)
            for i in range(per_owner):
                held[first + i] = piece[p, i].astype(jnp.float32) * scale[i : i + 1]
            first += per_owner
    chunk = 256
    row = lax.broadcasted_iota(jnp.int32, (8, chunk), 0)

    def variant(out, begin, v):
        places = [spots[4 * (begin + v) + k] for k in range(4)]
        offset = window_offsets[begin + v]
        for at in range(0, channels, chunk):
            lanes = slice(at, at + chunk)
            cells = [held[place, :, lanes] for place in places]
            delta = deltas32[pl.ds(begin + v, 1), lanes]
            cells[1] = cells[1] + jnp.where(row == offset, delta, 0.0)
            cells[2] = cells[2] + jnp.where(row == offset - 8, delta, 0.0)
            early, late = jnp.stack(cells[:3]), jnp.stack(cells[1:])
            total = early[0:2] * taps32[0, :, lanes]
            total = total + late[0:2] * (1.0 + taps32[8, :, lanes])
            total = total + late[1:3] * taps32[16, :, lanes]
            for s in range(1, 8):
                term = early * taps32[s, :, lanes] + late * taps32[s + 8, :, lanes]
                term = pltpu.roll(term.reshape(24, chunk), 24 - s, 0)
                total = total + term[:W].reshape(2, 8, chunk)
            out[pl.ds(pl.multiple_of(v * W, W), W), lanes] = total.reshape(W, chunk)

    begin = 0
    for out in outs:
        pl.loop(0, out.shape[0] // W)(functools.partial(variant, out, begin))
        begin += out.shape[0] // W


def value_window(h, value_width):
    return h * value_width // 128 * 128, -(-(h + 1) * value_width // 128) * 128


def row_starts(positions):
    return jnp.concatenate(
        [jnp.full((W, 1), positions[v], jnp.int32) for v in range(positions.shape[0])], axis=0
    ).astype(jnp.float32)


def scores_of(query, keys):
    product = lax.dot_general(
        query, keys, (((1,), (1,)), ((), ())), preferred_element_type=jnp.float32
    )
    return product * (1.0 / math.sqrt(query.shape[1]))


def key_places(piece, firsts):
    each = piece.shape[0] // len(firsts)
    places = [first + lax.broadcasted_iota(jnp.int32, (1, each), 1) for first in firsts]
    return jnp.concatenate(places, axis=1).astype(jnp.float32)


def piece_scores(h, query, start, place, slope, pieces, firsts):
    width, found = query.shape[1], []
    for piece, first in zip(pieces, firsts):
        key_at = key_places(piece, first)
        score = scores_of(query, piece[:, h * width : (h + 1) * width])
        score = score - slope * jnp.abs(place - key_at)
        kept = jnp.abs(start + (W - 1) / 2 - key_at) > W / 2
        found.append(jnp.where(kept, score, -jnp.inf))
    return found


def weigh(scores, values, peak):
    total, summed = 0.0, 0.0
    for score, value in zip(scores, values):
        weight = jnp.exp(score - peak)
        total = total + jnp.sum(weight, axis=1, keepdims=True)
        summed = summed + jnp.dot(
            weight.astype(jnp.bfloat16), value, preferred_element_type=jnp.float32
        )
    return total, summed


def peak_of(scores):
    return functools.reduce(jnp.maximum, [jnp.max(s, axis=1, keepdims=True) for s in scores])


def near_kernel(
    sizes,
    positions,
    slopes,
    gain,
    w_query,
    w_key,
    w_value,
    *rest,
):
    value_width, window_rows = sizes
    mine, others = rest[:PARTS], rest[PARTS : 2 * PARTS]
    pieces = rest[2 * PARTS : -3]
    queries_out, stats, sums = rest[-3:]
    heads = slopes.shape[0]
    rep = lax.axis_index("rep")
    own = jnp.concatenate([part[...] for part in mine], axis=0)
    far = jnp.concatenate([part[...] for part in others], axis=0)
    rows, half = own.shape
    mean = (
        jnp.sum(own * own, axis=1, keepdims=True) + jnp.sum(far * far, axis=1, keepdims=True)
    ) / (2 * half)
    factor = lax.rsqrt(mean + EPSILON)
    gain_low, gain_high = gain[:, :half], gain[:, half:]
    own = own * factor * jnp.where(rep == 0, gain_low, gain_high)
    far = far * factor * jnp.where(rep == 0, gain_high, gain_low)
    own, far = own.astype(jnp.bfloat16), far.astype(jnp.bfloat16)
    at_own = pl.ds(pl.multiple_of(rep * half, half), half)
    at_far = pl.ds(pl.multiple_of((1 - rep) * half, half), half)

    def project(w):
        return (
            jnp.dot(own, w[at_own, :], preferred_element_type=jnp.float32)
            + jnp.dot(far, w[at_far, :], preferred_element_type=jnp.float32)
        ).astype(jnp.bfloat16)

    queries, own_keys, own_values = project(w_query), project(w_key), project(w_value)
    queries_out[...] = queries
    start = row_starts(positions)
    place = start + (lax.broadcasted_iota(jnp.int32, (rows, 1), 0) % W).astype(jnp.float32)
    at = lax.broadcasted_iota(jnp.int32, (rows, rows), 0)
    to = lax.broadcasted_iota(jnp.int32, (rows, rows), 1)
    together, apart = at // W == to // W, jnp.abs(at - to).astype(jnp.float32)
    width = queries.shape[1] // heads
    for h in range(heads):
        cols = slice(h * width, (h + 1) * width)
        low, high = value_window(h, value_width)
        base = heads * width
        near = scores_of(queries[:, cols], own_keys[:, cols]) - slopes[h] * apart
        scores = [jnp.where(together, near, -jnp.inf)]
        scores += piece_scores(
            h, queries[:, cols], start, place, slopes[h], pieces, first_keys(window_rows)
        )
        values = [own_values[:, low:high]]
        values += [piece[:, base + low : base + high] for piece in pieces]
        peak = peak_of(scores)
        total, summed = weigh(scores, values, peak)
        stats[2 * h] = jnp.broadcast_to(peak, (rows, 128))
        stats[2 * h + 1] = jnp.broadcast_to(total, (rows, 128))
        sums[h] = summed


def spread(tile, width):
    return jnp.concatenate([tile] * (width // tile.shape[1]), axis=1)


def far_kernel(sizes, positions, slopes, queries, stats, sums, *rest):
    value_width, window_rows = sizes
    *pieces, out = rest
    firsts = first_keys(window_rows)[-len(pieces) :]
    heads = slopes.shape[0]
    rows, width = queries.shape[0], queries.shape[1] // heads
    start = row_starts(positions)
    place = start + (lax.broadcasted_iota(jnp.int32, (rows, 1), 0) % W).astype(jnp.float32)
    results = []
    for h in range(heads):
        low, high = value_window(h, value_width)
        base = heads * width
        scores = piece_scores(
            h,
            queries[:, h * width : (h + 1) * width],
            start,
            place,
            slopes[h],
            pieces,
            firsts,
        )
        values = [piece[:, base + low : base + high] for piece in pieces]
        before = stats[2 * h]
        peak = jnp.maximum(before, peak_of(scores))
        factor = jnp.exp(before - peak)
        total = stats[2 * h + 1] * factor
        summed = sums[h] * spread(factor, high - low)
        for score, value in zip(scores, values):
            weight = jnp.exp(score - spread(peak, score.shape[1]))
            total = total + jnp.sum(weight, axis=1, keepdims=True)
            summed = summed + jnp.dot(
                weight.astype(jnp.bfloat16), value, preferred_element_type=jnp.float32
            )
        results.append((low, high, summed * spread(1.0 / total, high - low)))
    lane = lax.broadcasted_iota(jnp.int32, (rows, 128), 1)
    for column in range(0, heads * value_width, 128):
        merged = None
        for h, (low, high, value) in enumerate(results):
            if low <= column < high:
                part = value[:, column - low : column - low + 128]
                if merged is None:
                    merged = part
                else:
                    merged = jnp.where(lane + column >= h * value_width, part, merged)
        out[:, column : column + 128] = merged.astype(jnp.bfloat16)


def on_device(
    cache_vals,
    cache_scales,
    block_slot,
    block_lists,
    variant_pos,
    window_offsets,
    variant_deltas,
    conv_taps,
    norm_gain,
    w_query,
    w_key,
    w_value,
    ref_keys,
    ref_values,
    head_slopes,
):
    per_owner, block_rows, channels = cache_vals.shape
    variants, per_variant = block_lists.shape
    half = channels // lax.axis_size("rep")
    smem = pl.BlockSpec(memory_space=pltpu.SMEM)
    vmem = pl.BlockSpec(memory_space=pltpu.VMEM)

    def my_half(x):
        return lax.dynamic_slice_in_dim(x, lax.axis_index("rep") * half, half, axis=x.ndim - 1)

    scales, vals = then(my_half(cache_scales), cache_vals)
    all_cells = per_owner + -(-per_owner // 8)
    cells = pl.pallas_call(
        pack_kernel,
        out_shape=jax.ShapeDtypeStruct((all_cells, block_rows, half), jnp.bfloat16),
        in_specs=[vmem, vmem],
        out_specs=vmem,
        compiler_params=pltpu.CompilerParams(vmem_limit_bytes=4 * 1024 * 1024),
        name="pack",
    )(my_half(vals), scales)
    window = jnp.concatenate([ref_keys, ref_values], axis=1)
    slot_pieces, window_pieces, (deltas, taps, gain) = gather_all(
        cells,
        window,
        my_half(variant_deltas),
        my_half(conv_taps),
        norm_gain.reshape(1, channels),
    )
    held = sum(piece.shape[0] for piece in slot_pieces) * per_owner
    tower_limit = 8 * held * block_rows * half * 4 // 3 + 4 * 1024 * 1024
    tower_shapes = [
        jax.ShapeDtypeStruct(((variants + i) // PARTS * W, half), jnp.float32)
        for i in reversed(range(PARTS))
    ]
    towers = pl.pallas_call(
        functools.partial(tower_kernel, per_owner),
        out_shape=tower_shapes,
        in_specs=[smem, smem, smem] + [vmem] * (2 + len(slot_pieces)),
        out_specs=[vmem] * PARTS,
        scratch_shapes=[
            pltpu.VMEM((held, block_rows, half), jnp.float32),
            pltpu.VMEM((TAPS, 8, half), jnp.float32),
            pltpu.VMEM((variants, half), jnp.float32),
            pltpu.SMEM((variants * per_variant,), jnp.int32),
        ],
        compiler_params=pltpu.CompilerParams(vmem_limit_bytes=tower_limit),
        cost_estimate=pl.CostEstimate(
            flops=10**9, bytes_accessed=4 * 10**7, transcendentals=0
        ),
        name="tower",
    )(
        block_slot,
        block_lists.T,
        window_offsets,
        deltas,
        taps,
        *slot_pieces,
    )
    swap = [(0, 1), (1, 0)]
    if len(window_pieces) > 2:
        *towers, window_pieces[4] = then(*towers, window_pieces[4])
        *towers, last = towers
        last, window_pieces[3] = then(last, window_pieces[3])
        towers = [*towers, last]
    others = [lax.ppermute(tower, "rep", swap) for tower in towers]
    heads, rows = head_slopes.shape[0], variants * W
    value_width = w_value.shape[1] // heads
    cut = len(window_pieces) - 1
    sizes = (value_width, ref_keys.shape[0])
    low, high = value_window(heads - 1, value_width)
    queries, stats, sums = pl.pallas_call(
        functools.partial(near_kernel, sizes),
        out_shape=[
            jax.ShapeDtypeStruct((rows, w_query.shape[1]), jnp.bfloat16),
            jax.ShapeDtypeStruct((2 * heads, rows, 128), jnp.float32),
            jax.ShapeDtypeStruct((heads, rows, high - low), jnp.float32),
        ],
        in_specs=[smem, smem] + [vmem] * (4 + 2 * PARTS + cut),
        out_specs=[vmem] * 3,
        compiler_params=pltpu.CompilerParams(vmem_limit_bytes=20 * 1024 * 1024),
        name="near",
    )(
        variant_pos,
        head_slopes,
        gain,
        w_query,
        w_key,
        w_value,
        *towers,
        *others,
        *window_pieces[:cut],
    )
    output = pl.pallas_call(
        functools.partial(far_kernel, sizes),
        out_shape=jax.ShapeDtypeStruct((rows, w_value.shape[1]), jnp.bfloat16),
        in_specs=[smem, smem] + [vmem] * (3 + len(window_pieces) - cut),
        out_specs=vmem,
        compiler_params=pltpu.CompilerParams(vmem_limit_bytes=20 * 1024 * 1024),
        name="far",
    )(variant_pos, head_slopes, queries, stats, sums, *window_pieces[cut:])
    return output.reshape(variants, W, -1)


def solution(mesh):
    placed = (
        P(("grp", "seq", "var"), None, None),
        P(("grp", "seq", "var"), None),
        P("grp"),
        P(("grp", "seq", "var"), None),
        P(("grp", "seq", "var")),
        P(("grp", "seq", "var")),
        P(("grp", "seq", "var"), None),
        P(),
        P(),
        P(None, "rep"),
        P(None, "rep"),
        P(None, "rep"),
        P(("grp", "seq"), "rep"),
        P(("grp", "seq"), "rep"),
        P("rep"),
    )
    return jax.shard_map(
        on_device,
        mesh=mesh,
        in_specs=placed,
        out_specs=P(("grp", "seq", "var"), None, "rep"),
        check_vma=False,
    )
```

```python
import functools
import math

import jax
import jax.numpy as jnp
from jax import lax
from jax.experimental import pallas as pl
from jax.experimental.pallas import tpu as pltpu
from jax.sharding import PartitionSpec as P

W = 16
RADIUS = 8
TAPS = 2 * RADIUS + 1
EPSILON = 1e-06
PARTS = 3


def send(x, seq_mask, var_mask=0):
    seq, var = lax.axis_size("seq"), lax.axis_size("var")
    pairs = [
        (p * var + q, (p ^ seq_mask) * var + (q ^ var_mask))
        for p in range(seq)
        for q in range(var)
    ]
    return lax.ppermute(x, ("seq", "var"), pairs)


def then(*arrays):
    return lax.optimization_barrier(arrays)


def pack_kernel(vals, scales, cells):
    per_owner, half = scales.shape
    cells[pl.ds(0, per_owner)] = vals[...]
    rows = scales[...].astype(jnp.float32)
    missing = (cells.shape[0] - per_owner) * 8 - per_owner
    if missing:
        rows = jnp.concatenate([rows, jnp.zeros((missing, half), jnp.float32)], axis=0)
    rows = rows.reshape(-1, 8, half).astype(jnp.bfloat16)
    cells[pl.ds(per_owner, rows.shape[0])] = rows


def gather_all(cells, window, *small):
    seq, var = lax.axis_size("seq"), lax.axis_size("var")
    me_var = lax.axis_index("var")
    if not on_line(seq, var):
        cells = lax.all_gather(cells, ("seq", "var"), axis=0, tiled=False)
        return [cells], [lax.all_gather(window, "seq", axis=0, tiled=True)], small
    part = window.shape[0] // 2

    cells_1, across, cells_3 = send(cells, 1), send(cells, 0, 1), send(cells, 3)
    cells_1, across, window = then(cells_1, across, window)
    share = lax.dynamic_slice_in_dim(window, me_var * part, part, axis=0)
    across_1 = send(cells_1, 0, 1)
    cells_3, *small = then(cells_3, *small)
    cells_2 = send(cells_3, 1)
    cells_3, across_1 = then(cells_3, across_1)
    across_3 = send(cells_3, 0, 1)
    cells_2, share = then(cells_2, share)
    across_2, share_3 = send(cells_2, 0, 1), send(share, 3)
    across_3, share_3, window = then(across_3, share_3, window)
    share_2, share_across_3 = send(share_3, 1), send(share_3, 0, 1)
    window_1, share_across_2 = send(window, 1), send(share_2, 0, 1)

    pieces = [cells, across, cells_1, across_1, cells_2, across_2, cells_3, across_3]
    windows = [window, window_1, share_3, share_across_3, share_2, share_across_2]
    return [piece[None] for piece in pieces], windows, small


def on_line(seq, var):
    return seq == 4 and var == 2


def place_of(owner):
    seq, var = lax.axis_size("seq"), lax.axis_size("var")
    if not on_line(seq, var):
        return owner
    return owner ^ (lax.axis_index("seq") * var + lax.axis_index("var"))


def first_keys(rows):
    seq, var = lax.axis_size("seq"), lax.axis_size("var")
    me_seq, me_var = lax.axis_index("seq"), lax.axis_index("var")
    if not on_line(seq, var):
        return [[rows * p for p in range(seq)]]
    firsts = [[me_seq * rows], [(me_seq ^ 1) * rows]]
    for mask in (3, 2):
        for side in (0, 1):
            firsts.append([(me_seq ^ mask) * rows + (me_var ^ side) * (rows // 2)])
    return firsts


def tower_kernel(
    per_owner,
    block_slot,
    block_lists,
    window_offsets,
    deltas,
    taps,
    *rest,
):
    *rest, held, taps32, deltas32, spots = rest
    pieces, outs = rest[:-PARTS], rest[-PARTS:]
    channels = taps32.shape[2]
    for v in range(block_lists.shape[1]):
        for k in range(4):
            slot = block_slot[block_lists[k, v]]
            owner = lax.div(slot, per_owner)
            spots[4 * v + k] = place_of(owner) * per_owner + lax.rem(slot, per_owner)
    taps32[...] = jnp.broadcast_to(taps[...].astype(jnp.float32)[:, None, :], taps32.shape)
    deltas32[...] = deltas[...].astype(jnp.float32)
    first = 0
    for piece in pieces:
        scale_cells = piece.shape[1] - per_owner
        for p in range(piece.shape[0]):
            scale = piece[p, pl.ds(per_owner, scale_cells)].astype(jnp.float32)
            scale = scale.reshape(scale_cells * 8, channels)
            for i in range(per_owner):
                held[first + i] = piece[p, i].astype(jnp.float32) * scale[i : i + 1]
            first += per_owner
    chunk = 256
    row = lax.broadcasted_iota(jnp.int32, (8, chunk), 0)

    def variant(out, begin, v):
        places = [spots[4 * (begin + v) + k] for k in range(4)]
        offset = window_offsets[begin + v]
        for at in range(0, channels, chunk):
            lanes = slice(at, at + chunk)
            cells = [held[place, :, lanes] for place in places]
            delta = deltas32[pl.ds(begin + v, 1), lanes]
            cells[1] = cells[1] + jnp.where(row == offset, delta, 0.0)
            cells[2] = cells[2] + jnp.where(row == offset - 8, delta, 0.0)
            early, late = jnp.stack(cells[:3]), jnp.stack(cells[1:])
            total = early[0:2] * taps32[0, :, lanes]
            total = total + late[0:2] * (1.0 + taps32[8, :, lanes])
            total = total + late[1:3] * taps32[16, :, lanes]
            for s in range(1, 8):
                term = early * taps32[s, :, lanes] + late * taps32[s + 8, :, lanes]
                term = pltpu.roll(term.reshape(24, chunk), 24 - s, 0)
                total = total + term[:W].reshape(2, 8, chunk)
            out[pl.ds(pl.multiple_of(v * W, W), W), lanes] = total.reshape(W, chunk)

    begin = 0
    for out in outs:
        pl.loop(0, out.shape[0] // W, unroll=True)(functools.partial(variant, out, begin))
        begin += out.shape[0] // W


def value_window(h, value_width):
    return h * value_width // 128 * 128, -(-(h + 1) * value_width // 128) * 128


def row_starts(positions):
    return jnp.concatenate(
        [jnp.full((W, 1), positions[v], jnp.int32) for v in range(positions.shape[0])], axis=0
    ).astype(jnp.float32)


def scores_of(query, keys):
    product = lax.dot_general(
        query, keys, (((1,), (1,)), ((), ())), preferred_element_type=jnp.float32
    )
    return product * (1.0 / math.sqrt(query.shape[1]))


def key_places(piece, firsts):
    each = piece.shape[0] // len(firsts)
    places = [first + lax.broadcasted_iota(jnp.int32, (1, each), 1) for first in firsts]
    return jnp.concatenate(places, axis=1).astype(jnp.float32)


def piece_scores(h, query, start, place, slope, pieces, firsts):
    width, found = query.shape[1], []
    for piece, first in zip(pieces, firsts):
        key_at = key_places(piece, first)
        score = scores_of(query, piece[:, h * width : (h + 1) * width])
        score = score - slope * jnp.abs(place - key_at)
        kept = jnp.abs(start + (W - 1) / 2 - key_at) > W / 2
        found.append(jnp.where(kept, score, -jnp.inf))
    return found


def weigh(scores, values, peak):
    total, summed = 0.0, 0.0
    for score, value in zip(scores, values):
        weight = jnp.exp(score - peak)
        total = total + jnp.sum(weight, axis=1, keepdims=True)
        summed = summed + jnp.dot(
            weight.astype(jnp.bfloat16), value, preferred_element_type=jnp.float32
        )
    return total, summed


def peak_of(scores):
    return functools.reduce(jnp.maximum, [jnp.max(s, axis=1, keepdims=True) for s in scores])


def near_kernel(
    sizes,
    positions,
    slopes,
    gain,
    w_query,
    w_key,
    w_value,
    *rest,
):
    value_width, window_rows = sizes
    mine, others = rest[:PARTS], rest[PARTS : 2 * PARTS]
    pieces = rest[2 * PARTS : -3]
    queries_out, stats, sums = rest[-3:]
    heads = slopes.shape[0]
    rep = lax.axis_index("rep")
    own = jnp.concatenate([part[...] for part in mine], axis=0)
    far = jnp.concatenate([part[...] for part in others], axis=0)
    rows, half = own.shape
    mean = (
        jnp.sum(own * own, axis=1, keepdims=True) + jnp.sum(far * far, axis=1, keepdims=True)
    ) / (2 * half)
    factor = lax.rsqrt(mean + EPSILON)
    gain_low, gain_high = gain[:, :half], gain[:, half:]
    own = own * factor * jnp.where(rep == 0, gain_low, gain_high)
    far = far * factor * jnp.where(rep == 0, gain_high, gain_low)
    own, far = own.astype(jnp.bfloat16), far.astype(jnp.bfloat16)
    at_own = pl.ds(pl.multiple_of(rep * half, half), half)
    at_far = pl.ds(pl.multiple_of((1 - rep) * half, half), half)

    def project(w):
        return (
            jnp.dot(own, w[at_own, :], preferred_element_type=jnp.float32)
            + jnp.dot(far, w[at_far, :], preferred_element_type=jnp.float32)
        ).astype(jnp.bfloat16)

    queries, own_keys, own_values = project(w_query), project(w_key), project(w_value)
    queries_out[...] = queries
    start = row_starts(positions)
    place = start + (lax.broadcasted_iota(jnp.int32, (rows, 1), 0) % W).astype(jnp.float32)
    at = lax.broadcasted_iota(jnp.int32, (rows, rows), 0)
    to = lax.broadcasted_iota(jnp.int32, (rows, rows), 1)
    together, apart = at // W == to // W, jnp.abs(at - to).astype(jnp.float32)
    width = queries.shape[1] // heads
    for h in range(heads):
        cols = slice(h * width, (h + 1) * width)
        low, high = value_window(h, value_width)
        base = heads * width
        near = scores_of(queries[:, cols], own_keys[:, cols]) - slopes[h] * apart
        scores = [jnp.where(together, near, -jnp.inf)]
        scores += piece_scores(
            h, queries[:, cols], start, place, slopes[h], pieces, first_keys(window_rows)
        )
        values = [own_values[:, low:high]]
        values += [piece[:, base + low : base + high] for piece in pieces]
        peak = peak_of(scores)
        total, summed = weigh(scores, values, peak)
        stats[2 * h] = jnp.broadcast_to(peak, (rows, 128))
        stats[2 * h + 1] = jnp.broadcast_to(total, (rows, 128))
        sums[h] = summed


def spread(tile, width):
    return jnp.concatenate([tile] * (width // tile.shape[1]), axis=1)


def far_kernel(sizes, positions, slopes, queries, stats, sums, *rest):
    value_width, window_rows = sizes
    *pieces, out = rest
    firsts = first_keys(window_rows)[-len(pieces) :]
    heads = slopes.shape[0]
    rows, width = queries.shape[0], queries.shape[1] // heads
    start = row_starts(positions)
    place = start + (lax.broadcasted_iota(jnp.int32, (rows, 1), 0) % W).astype(jnp.float32)
    results = []
    for h in range(heads):
        low, high = value_window(h, value_width)
        base = heads * width
        scores = piece_scores(
            h,
            queries[:, h * width : (h + 1) * width],
            start,
            place,
            slopes[h],
            pieces,
            firsts,
        )
        values = [piece[:, base + low : base + high] for piece in pieces]
        before = stats[2 * h]
        peak = jnp.maximum(before, peak_of(scores))
        factor = jnp.exp(before - peak)
        total = stats[2 * h + 1] * factor
        summed = sums[h] * spread(factor, high - low)
        for score, value in zip(scores, values):
            weight = jnp.exp(score - spread(peak, score.shape[1]))
            total = total + jnp.sum(weight, axis=1, keepdims=True)
            summed = summed + jnp.dot(
                weight.astype(jnp.bfloat16), value, preferred_element_type=jnp.float32
            )
        results.append((low, high, summed * spread(1.0 / total, high - low)))
    lane = lax.broadcasted_iota(jnp.int32, (rows, 128), 1)
    for column in range(0, heads * value_width, 128):
        merged = None
        for h, (low, high, value) in enumerate(results):
            if low <= column < high:
                part = value[:, column - low : column - low + 128]
                if merged is None:
                    merged = part
                else:
                    merged = jnp.where(lane + column >= h * value_width, part, merged)
        out[:, column : column + 128] = merged.astype(jnp.bfloat16)


def on_device(
    cache_vals,
    cache_scales,
    block_slot,
    block_lists,
    variant_pos,
    window_offsets,
    variant_deltas,
    conv_taps,
    norm_gain,
    w_query,
    w_key,
    w_value,
    ref_keys,
    ref_values,
    head_slopes,
):
    per_owner, block_rows, channels = cache_vals.shape
    variants, per_variant = block_lists.shape
    half = channels // lax.axis_size("rep")
    smem = pl.BlockSpec(memory_space=pltpu.SMEM)
    vmem = pl.BlockSpec(memory_space=pltpu.VMEM)

    def my_half(x):
        return lax.dynamic_slice_in_dim(x, lax.axis_index("rep") * half, half, axis=x.ndim - 1)

    scales, vals = then(my_half(cache_scales), cache_vals)
    all_cells = per_owner + -(-per_owner // 8)
    cells = pl.pallas_call(
        pack_kernel,
        out_shape=jax.ShapeDtypeStruct((all_cells, block_rows, half), jnp.bfloat16),
        in_specs=[vmem, vmem],
        out_specs=vmem,
        compiler_params=pltpu.CompilerParams(vmem_limit_bytes=4 * 1024 * 1024),
        name="pack",
    )(my_half(vals), scales)
    window = jnp.concatenate([ref_keys, ref_values], axis=1)
    slot_pieces, window_pieces, (deltas, taps, gain) = gather_all(
        cells,
        window,
        my_half(variant_deltas),
        my_half(conv_taps),
        norm_gain.reshape(1, channels),
    )
    held = sum(piece.shape[0] for piece in slot_pieces) * per_owner
    tower_limit = 8 * held * block_rows * half * 4 // 3 + 4 * 1024 * 1024
    tower_shapes = [
        jax.ShapeDtypeStruct(((variants + i) // PARTS * W, half), jnp.float32)
        for i in reversed(range(PARTS))
    ]
    towers = pl.pallas_call(
        functools.partial(tower_kernel, per_owner),
        out_shape=tower_shapes,
        in_specs=[smem, smem, smem] + [vmem] * (2 + len(slot_pieces)),
        out_specs=[vmem] * PARTS,
        scratch_shapes=[
            pltpu.VMEM((held, block_rows, half), jnp.float32),
            pltpu.VMEM((TAPS, 8, half), jnp.float32),
            pltpu.VMEM((variants, half), jnp.float32),
            pltpu.SMEM((variants * per_variant,), jnp.int32),
        ],
        compiler_params=pltpu.CompilerParams(vmem_limit_bytes=tower_limit),
        cost_estimate=pl.CostEstimate(
            flops=10**9, bytes_accessed=4 * 10**7, transcendentals=0
        ),
        name="tower",
    )(
        block_slot,
        block_lists.T,
        window_offsets,
        deltas,
        taps,
        *slot_pieces,
    )
    swap = [(0, 1), (1, 0)]
    if len(window_pieces) > 2:
        *towers, window_pieces[4] = then(*towers, window_pieces[4])
        *towers, last = towers
        last, window_pieces[3] = then(last, window_pieces[3])
        towers = [*towers, last]
    others = [lax.ppermute(tower, "rep", swap) for tower in towers]
    heads, rows = head_slopes.shape[0], variants * W
    value_width = w_value.shape[1] // heads
    cut = len(window_pieces) - 1
    sizes = (value_width, ref_keys.shape[0])
    low, high = value_window(heads - 1, value_width)
    queries, stats, sums = pl.pallas_call(
        functools.partial(near_kernel, sizes),
        out_shape=[
            jax.ShapeDtypeStruct((rows, w_query.shape[1]), jnp.bfloat16),
            jax.ShapeDtypeStruct((2 * heads, rows, 128), jnp.float32),
            jax.ShapeDtypeStruct((heads, rows, high - low), jnp.float32),
        ],
        in_specs=[smem, smem] + [vmem] * (4 + 2 * PARTS + cut),
        out_specs=[vmem] * 3,
        compiler_params=pltpu.CompilerParams(vmem_limit_bytes=20 * 1024 * 1024),
        name="near",
    )(
        variant_pos,
        head_slopes,
        gain,
        w_query,
        w_key,
        w_value,
        *towers,
        *others,
        *window_pieces[:cut],
    )
    output = pl.pallas_call(
        functools.partial(far_kernel, sizes),
        out_shape=jax.ShapeDtypeStruct((rows, w_value.shape[1]), jnp.bfloat16),
        in_specs=[smem, smem] + [vmem] * (3 + len(window_pieces) - cut),
        out_specs=vmem,
        compiler_params=pltpu.CompilerParams(vmem_limit_bytes=20 * 1024 * 1024),
        name="far",
    )(variant_pos, head_slopes, queries, stats, sums, *window_pieces[cut:])
    return output.reshape(variants, W, -1)


def solution(mesh):
    placed = (
        P(("grp", "seq", "var"), None, None),
        P(("grp", "seq", "var"), None),
        P("grp"),
        P(("grp", "seq", "var"), None),
        P(("grp", "seq", "var")),
        P(("grp", "seq", "var")),
        P(("grp", "seq", "var"), None),
        P(),
        P(),
        P(None, "rep"),
        P(None, "rep"),
        P(None, "rep"),
        P(("grp", "seq"), "rep"),
        P(("grp", "seq"), "rep"),
        P("rep"),
    )
    return jax.shard_map(
        on_device,
        mesh=mesh,
        in_specs=placed,
        out_specs=P(("grp", "seq", "var"), None, "rep"),
        check_vma=False,
    )
```
